1024 devices in a mesh: dp: 32 (over z, core), node: 4 (over x), local: 8 (over y).
Axes of the slice: x: 4, y: 8, z: 16, core: 2. Of those that a mesh axis runs over, the one named last changes fastest.
Arguments:
- grad_out: bfloat16 [131072, 7168], P(('dp', 'node', 'local')), parts along dimension 0, may hold values from -6 to 6
- probs: float32 [131072], P(('dp', 'node', 'local')), parts along dimension 0, may hold values from 0.05 to 1
- expert_ids: int32 [131072], P(('dp', 'node', 'local')), parts along dimension 0, may hold values from 0 to 3, as said below
- slot_ids: int32 [131072], P(('dp', 'node', 'local')), parts along dimension 0, may hold values from 0 to 33
- w_down: bfloat16 [4, 2048, 7168], P('node', None, 'local'), may hold values from -0.125 to 0.125
- hidden: bfloat16 [128, 2048, 1088], P(('dp', 'node'), 'local'), parts along dimension 0, may hold values from -0.29882812 to 0.29882812
Outputs:
- d_hidden: bfloat16 [128, 2048, 1088], P(('dp', 'node'), 'local'), parts along dimension 0
- d_probs: float32 [131072], P(('dp', 'node', 'local')), parts along dimension 0
The draws below stay inside these ranges and needn't reach their ends.
There are 32 independent parts, one for each index of `dp`. The reference program is written for one: setup_inputs(seed, part) draws one part's arguments, and reference() takes and returns one part's arrays. A program takes and returns all parts, laid end to end along the dimension named above; an argument that names none is the same for every part. Nothing has to cross between parts.
Inputs may be any that keep to these rules, and one draw needn't show every extreme that they name: `expert_ids`: among the tokens of one device no two share both expert and slot; every expert receives tokens of every device, and in every draw one expert receives 34 tokens of every device.
All inputs are finite; a program needn't handle non-finite values.
Results may differ from the reference program's by a relative error of at most 0.02.
Values may be sent and summed in bfloat16 or wider, within the bound.
A program may use at most 32 MiB of HBM per device.

```python
import math
import jax
import jax.numpy as jnp
from jax import lax

D = 7168
FF = 2048
TOK_DEV = 128
EXPERTS = 4
TOKENS = 4096
SLOT_CAP = 34
CAP = 1088
N_LOCAL = 8


def route_table(key):
    favoured = jax.random.randint(jax.random.fold_in(key, 7), (), 0, EXPERTS)
    blocks = TOKENS // TOK_DEV
    keys = jax.random.split(jax.random.fold_in(key, 11), blocks)

    def one_block(block_key):
        first_key, second_key = jax.random.split(block_key)
        table = jax.random.permutation(first_key, EXPERTS * SLOT_CAP).astype(jnp.int32)
        order = jnp.argsort((table // SLOT_CAP != favoured).astype(jnp.int32), stable=True)
        table = table[order][:TOK_DEV]
        placed = jax.random.permutation(second_key, TOK_DEV)
        return jnp.zeros((TOK_DEV,), jnp.int32).at[placed].set(table)
    return jax.vmap(one_block)(keys).reshape(-1)


def draw_expert_ids(key, part):
    table = route_table(key)
    return (table // SLOT_CAP).astype(jnp.int32)


def draw_slot_ids(key, part):
    table = route_table(key)
    return (table % SLOT_CAP).astype(jnp.int32)


def block_levels(key, extent, cuts, least, high):
    loudness, own = 1.0, jax.random.fold_in(key, 6)
    for axis_at, parts in cuts:
        heights = jnp.exp(jax.random.uniform(jax.random.fold_in(own, axis_at), (parts,), jnp.float32, least / len(cuts), high / len(cuts)))
        loudness = loudness * jnp.repeat(heights, extent[axis_at] // parts).reshape([-1 if axis == axis_at else 1 for axis in range(len(extent))])
    return loudness


def centred(stream_key, extent, spread, most, cuts=(), kind=jnp.bfloat16):
    loudness = block_levels(stream_key, extent, cuts, -0.22, 0.18) if cuts else 1.0
    result = jax.random.normal(stream_key, extent, jnp.float32) * spread * loudness
    return jnp.minimum(jnp.maximum(result, -most), most).astype(kind)


def setup_inputs(seed: int = 0, part: int = 0) -> dict:
    key_of = jax.random.split(jax.random.key(seed), 7)
    part_splits = jax.random.split(jax.random.fold_in(key_of[6], part), 7)
    return {
        "grad_out": centred(part_splits[0], (TOKENS, D), 1.0, 6.0, ((0, 32),)),
        "probs": jnp.clip(jnp.exp(math.log(1.0) - 2.9957323 * jax.random.uniform(part_splits[1], (TOKENS,), jnp.float32) ** block_levels(part_splits[1], (TOKENS,), ((0, 32),), -0.2, 0.2)), 0.05, 1.0),
        "expert_ids": draw_expert_ids(jax.random.fold_in(jax.random.fold_in(key_of[6], part), 71), part),
        "slot_ids": draw_slot_ids(jax.random.fold_in(jax.random.fold_in(key_of[6], part), 71), part),
        "w_down": centred(key_of[4], (EXPERTS, FF, D), FF ** -0.5, 0.125, ((0, 4), (2, 8))),
        "hidden": centred(part_splits[5], (EXPERTS, FF, CAP), 0.05, 0.29882812, ((0, 4), (1, 8))),
    }


def reference(grad_out, probs, expert_ids, slot_ids, w_down, hidden):
    source = jnp.arange(TOKENS, dtype=jnp.int32) // TOK_DEV
    cell = (source * SLOT_CAP + slot_ids).astype(jnp.int32)
    dispatched = jnp.zeros((EXPERTS, CAP, D), jnp.bfloat16).at[expert_ids, cell].set(grad_out)
    weights = jnp.zeros((EXPERTS, CAP), jnp.float32).at[expert_ids, cell].set(
        probs.astype(jnp.bfloat16).astype(jnp.float32))

    def per_expert(pack):
        weight, rows, wts, saved = pack
        blocks_w = weight.astype(jnp.float32).reshape(FF, N_LOCAL, D // N_LOCAL)
        blocks_r = rows.astype(jnp.float32).reshape(CAP, N_LOCAL, D // N_LOCAL)
        partial_terms = jnp.einsum("fld,cld->lfc", blocks_w, blocks_r)
        raw = jnp.sum(partial_terms.astype(jnp.bfloat16).astype(jnp.float32), axis=0)
        grad_h = (wts[None, :] * raw).astype(jnp.bfloat16)
        route = jnp.sum(saved.astype(jnp.float32) * raw, axis=0)
        return grad_h, route

    d_hidden, route_grad = lax.map(per_expert, (w_down, dispatched, weights, hidden))
    d_probs = route_grad[expert_ids, cell]
    return d_hidden, d_probs
```

```python
import functools

import jax
import jax.numpy as jnp
import numpy as np
from jax import lax
from jax.experimental import pallas as pl
from jax.experimental.pallas import tpu as pltpu
from jax.sharding import PartitionSpec as P

MESH = pl.DeviceIdType.MESH
BF = jnp.bfloat16
F32 = jnp.float32
ROUNDS = 4
STAGGER = 3
NT = (((1,), (1,)), ((), ()))


def kernel(NX, NY, NZ, per, BL, grad_h, eid_ref, sid_ref, prob_ref, tab_ref, w_h, hid_h,
           dh_ref, dp_ref,
           grad_v, w_v, hid_v, sendx, rx, swap, tok, wbuf, rets, retr, own, outs, res, wpad, perm,
           msgs, back,
           load_sem, yf_send, ring_send, ring_sem, sib_sem, xs_sem, xr_sem, sw_send, sw_recv,
           rt_send, rt_recv, out_send, out_recv, pb_send, pb_recv):
    NB = NY // 2
    NI = NY // 4
    CR = NI * 128 // NZ
    SL = 48
    C0 = NX * per
    CP = -(-(C0 + NX) // 16) * 16
    CA = -(-(CP // 2) // 16) * 16
    CELLS = NX * NY * per
    half = NZ // 2

    x = lax.axis_index("node")
    y = lax.axis_index("local")
    dp = lax.axis_index("dp")
    z = lax.div(dp, 2)
    k = lax.rem(dp, 2)
    par = lax.rem(y, 2)
    sib = {"dp": dp + 1 - 2 * k}
    z_up = {"dp": lax.rem(z + 1, NZ) * 2 + k}
    z_dn = {"dp": lax.rem(z + NZ - 1, NZ) * 2 + k}
    y_up = {"local": lax.rem(y + 1, NY)}
    y_dn = {"local": lax.rem(y + NY - 1, NY)}

    def remote(src, dst, ss, rs, dev):
        pltpu.make_async_remote_copy(src_ref=src, dst_ref=dst, send_sem=ss, recv_sem=rs,
                                     device_id=dev, device_id_type=MESH).start()

    def await_bytes(ref, sem):
        pltpu.make_async_copy(ref, ref, sem).wait()

    g_copy = pltpu.make_async_copy(grad_h, grad_v, load_sem.at[0])
    g_copy.start()
    w_copy = pltpu.make_async_copy(w_h, w_v, load_sem.at[1])
    w_copy.start()
    h_copy = pltpu.make_async_copy(hid_h, hid_v, load_sem.at[2])
    h_copy.start()

    bar = pltpu.get_barrier_semaphore()
    group = NX * NY
    mine = x * NY + y

    def greet(i, _):
        p = lax.rem(mine + i, group)
        pl.semaphore_signal(bar, inc=1, device_id={"node": lax.div(p, NY), "local": lax.rem(p, NY)},
                            device_id_type=MESH)
        return 0

    for dev in (z_up, z_dn, sib):
        pl.semaphore_signal(bar, inc=1, device_id=dev, device_id_type=MESH)
    lax.fori_loop(1, group, greet, 0)
    pl.semaphore_wait(bar, group - 1 + 3)

    for r in range(ROUNDS):
        at = z * CR
        row = (NB * k + 2 * lax.div(at, 128) + r % 2) * 256 + 128 * (r // 2) + lax.rem(at, 128)
        row = pl.multiple_of(row, 16)
        for j in range(1, NB):
            remote(w_h.at[pl.ds(row, CR)], wbuf.at[(r * 2 + k) * NZ + z, j - 1], yf_send,
                   ring_sem.at[r * NZ + z], {"local": lax.rem(y + NY - 2 * j, NY)})

    g_copy.wait()
    eid, sid = eid_ref[...], sid_ref[...]
    prow = jnp.broadcast_to(prob_ref[...], (16, prob_ref.shape[1])).astype(BF)
    T = eid.shape[1]
    rows_sl = lax.broadcasted_iota(jnp.int32, (SL, T), 0)
    rows_w = lax.broadcasted_iota(jnp.int32, (128, T), 0)
    rows_sl2 = lax.broadcasted_iota(jnp.int32, (SL, 128), 0)
    hot, wts = [], []
    for i in range(NX):
        e = lax.rem(x + i, NX)
        hot.append(jnp.where((eid == e) & (sid == rows_sl), 1.0, 0.0))
        hot_w = jnp.where((eid == e) & (sid == rows_w), 1.0, 0.0).astype(BF)
        wt = lax.dot_general(prow, hot_w, NT, preferred_element_type=F32)[0:1]
        wts.append(jnp.where(rows_sl2 == per, jnp.broadcast_to(wt, (SL, 128)), 0.0))
    hot = jnp.concatenate(hot, axis=0).astype(BF)
    wts = jnp.concatenate(wts, axis=0)
    for ph in range(2):
        pp = 1 - par if ph == 0 else par
        for jj in range(NB):
            b = 2 * jj + pp
            lanes = pl.ds(pl.multiple_of(b * BL, 128), BL)
            val = jnp.dot(hot, grad_v[:, lanes], preferred_element_type=F32)
            first = (val[:, 0:128] + wts).astype(BF)
            val = val.astype(BF)
            pj = pp * NB + jj
            for i in range(NX):
                cut = slice(SL * i, SL * (i + 1))
                if i == 0:
                    rx[pj, x] = val[cut]
                    rx[pj, x, :, 0:128] = first[cut]
                else:
                    sendx[i - 1, pj] = val[cut]
                    sendx[i - 1, pj, :, 0:128] = first[cut]
        for i in range(1, NX):
            remote(sendx.at[i - 1, pl.ds(pp * NB, NB)], rx.at[pl.ds(pp * NB, NB), x], xs_sem,
                   xr_sem.at[ph], {"node": lax.rem(x + i, NX)})

    def ring(r, d):
        base = (r * 2 + k) * NZ

        def chunk(src):
            await_bytes(wbuf.at[base + src], ring_sem.at[r * NZ + src])

        def pass_on(src, dev):
            remote(wbuf.at[base + src], wbuf.at[base + src], ring_send.at[r],
                   ring_sem.at[r * NZ + src], dev)

        def to_sibling(src):
            remote(wbuf.at[base + src], wbuf.at[base + src], ring_send.at[r], sib_sem.at[r], sib)

        d_up = half if r % 2 == 0 else half - 1
        d_dn = NZ - 1 - d_up
        if d == 0:
            chunk(z)
            if d_up > 0:
                pass_on(z, z_up)
            if d_dn > 0:
                pass_on(z, z_dn)
            to_sibling(z)
            return
        for up in (True, False):
            reach = d_up if up else d_dn
            if d > reach:
                continue
            src = lax.rem(z + NZ - d, NZ) if up else lax.rem(z + d, NZ)
            chunk(src)
            if d < reach:
                pass_on(src, z_up if up else z_dn)
            to_sibling(src)

    def compact(ph):
        q = lax.broadcasted_iota(jnp.int32, (CP, NX * SL), 0)
        c = lax.broadcasted_iota(jnp.int32, (CP, NX * SL), 1)
        keep = q < 0
        for n in range(NX):
            keep = keep | ((q >= per * n) & (q < per * (n + 1)) & (c - SL * n == q - per * n))
            keep = keep | ((q == C0 + n) & (c == SL * n + per))
        pick = jnp.where(keep, 1.0, 0.0).astype(BF)
        await_bytes(sendx.at[:, pl.ds(0, NB)], xr_sem.at[ph])
        pp = 1 - par if ph == 0 else par
        for j in range(NB):
            jj = j if ph == 0 else lax.div(lax.rem(y + 2 * j, NY), 2)
            got = rx[pp * NB + jj].reshape(NX * SL, BL)
            val = jnp.dot(pick, got, preferred_element_type=F32).astype(BF)
            if ph == 0:
                swap[jj] = val
            else:
                tok[j, 0:CP] = val
                if j == 0:
                    wpad[...] = val[:, 0:128]
        if ph == 0:
            for j in range(NB):
                lo = lax.div(lax.rem(y + NY - 1 + 2 * j, NY), 2)
                hi = lax.div(lax.rem(y + 1 + 2 * j, NY), 2)
                remote(swap.at[lo, pl.ds(0, CA)], tok.at[j, pl.ds(CP, CA)], sw_send, sw_recv, y_dn)
                remote(swap.at[hi, pl.ds(CA, CP - CA)], tok.at[j, pl.ds(CP + CA, CP - CA)],
                       sw_send, sw_recv, y_up)

    def compute(r):
        await_bytes(wbuf.at[pl.ds((r * 2 + 1 - k) * NZ, NZ)], sib_sem.at[r])
        for kk in range(2):
            own_w = [w_v[pl.ds((NB * kk + 2 * i + r % 2) * 256 + 128 * (r // 2), 128), :]
                     for i in range(NI)]
            own_w = jnp.concatenate(own_w, axis=0) if NI > 1 else own_w[0]
            acc = lax.dot_general(tok[0], own_w, NT, preferred_element_type=F32)
            for j in range(1, NB):
                wj = wbuf[(r * 2 + kk) * NZ:(r * 2 + kk + 1) * NZ, j - 1].reshape(NI * 128, BL)
                acc = acc + lax.dot_general(tok[j], wj, NT, preferred_element_type=F32)
            own[kk] = acc[0:CP]
            m = r * 2 + kk
            rets[m] = acc[CP:2 * CP].astype(BF)
            remote(rets.at[m, pl.ds(0, CA)], retr.at[m, pl.ds(0, CA)], rt_send, rt_recv.at[m], y_up)
            remote(rets.at[m, pl.ds(CA, CP - CA)], retr.at[m, pl.ds(CA, CP - CA)], rt_send,
                   rt_recv.at[m], y_dn)

    def finish(r):
        h = r // 2
        rows = lax.broadcasted_iota(jnp.int32, (CP, 128), 0)
        for kk in range(2):
            m = r * 2 + kk
            await_bytes(retr.at[m], rt_recv.at[m])
            for i in range(NI):
                cut = slice(128 * i, 128 * (i + 1))
                val = own[kk, :, cut] + retr[m, :, cut].astype(F32)
                val = jnp.where(rows >= C0, wpad[...].astype(F32), val).astype(BF)
                dest = NB * kk + 2 * i + r % 2
                slot = m * NI + i
                outs[slot] = val

                @pl.when(y != dest)
                def _():
                    remote(outs.at[slot], res.at[h * NY + y], out_send, out_recv.at[h],
                           {"local": jnp.int32(dest)})

                @pl.when(y == dest)
                def _():
                    res[h * NY + dest] = val

    def tail(h):
        await_bytes(res.at[pl.ds(0, NY - 1)], out_recv.at[h])
        got = res[h * NY:(h + 1) * NY]
        raw = lax.dot_general(got.reshape(NY * CP, 128), perm[...], (((0,), (0,)), ((), ())),
                              preferred_element_type=F32)
        s_row = tab_ref[2:3, :]
        spread = jnp.where(lax.broadcasted_iota(jnp.int32, (128, CELLS), 0) == s_row, 1.0, 0.0)
        last = C0 // 16 * 16
        sheet = got[:, last:last + 16, :].reshape(NY * 16, 128)
        wide = jnp.dot(sheet, spread.astype(BF), preferred_element_type=F32)
        mine_row = lax.broadcasted_iota(jnp.int32, (NY * 16, CELLS), 0)
        w_row = jnp.sum(jnp.where(mine_row == tab_ref[3:4, :], wide, 0.0), axis=0, keepdims=True)
        dh_ref[pl.ds(128 * h, 128), :] = (raw * w_row).astype(BF)
        saved = hid_v[pl.ds(128 * h, 128), :].astype(F32)
        return jnp.sum(saved * raw, axis=0, keepdims=True)

    def build_perm():
        for l in range(NY):
            q = lax.broadcasted_iota(jnp.int32, (CP, CELLS), 0) + l * CP
            perm[l * CP:(l + 1) * CP, :] = jnp.where(q == tab_ref[0:1, :], 1.0, 0.0).astype(BF)

    last_t = half + STAGGER * (ROUNDS - 1)
    route = None
    for t in range(last_t + 1):
        for r in range(ROUNDS):
            if 0 <= t - STAGGER * r <= half:
                ring(r, t - STAGGER * r)
        if t == min(1, last_t):
            build_perm()
            w_copy.wait()
            h_copy.wait()
        if t == half // 2:
            compact(0)
        if t == half - 1:
            compact(1)
        if t == half:
            await_bytes(tok.at[:, pl.ds(CP, CP)], sw_recv)
        for r in range(ROUNDS):
            done = half + STAGGER * r
            if t == done:
                compute(r)
                if r == ROUNDS - 1:
                    finish(r)
            elif t == done + 1:
                finish(r)
    route = tail(0) + tail(1)

    src_rows = lax.broadcasted_iota(jnp.int32, (group, CELLS), 0)
    split = jnp.where(src_rows == tab_ref[1:2, :], jnp.broadcast_to(route, (group, CELLS)), 0.0)
    spread = jnp.where(lax.broadcasted_iota(jnp.int32, (128, CELLS), 0) == tab_ref[2:3, :], 1.0, 0.0)
    rows = lax.dot_general(split, spread, NT, preferred_element_type=F32,
                           precision=lax.Precision.HIGHEST)
    msgs[...] = jnp.broadcast_to(rows[:, None, :], (group, 8, 128))
    back[mine] = msgs[mine]

    def give(i, _):
        p = lax.rem(mine + i, group)
        remote(msgs.at[p], back.at[mine], pb_send, pb_recv,
               {"node": lax.div(p, NY), "local": lax.rem(p, NY)})
        return 0

    lax.fori_loop(1, group, give, 0)
    await_bytes(back.at[pl.ds(0, group - 1)], pb_recv)
    sums = [jnp.sum(back[e * NY:(e + 1) * NY], axis=0)[0:1] for e in range(NX)]
    slot_hot = jnp.where(sid == rows_w, 1.0, 0.0)
    total = jnp.zeros((8, T), F32)
    for e in range(NX):
        got = jnp.dot(jnp.broadcast_to(sums[e], (8, 128)), slot_hot, preferred_element_type=F32,
                      precision=lax.Precision.HIGHEST)
        total = total + jnp.where(eid == e, got, 0.0)
    dp_ref[...] = total

    await_bytes(wbuf.at[pl.ds(0, ROUNDS * (NB - 1)), 0], yf_send)
    for r in range(ROUNDS):
        await_bytes(wbuf.at[pl.ds(0, 2 * NZ - 1)], ring_send.at[r])
    await_bytes(sendx, xs_sem)
    await_bytes(tok.at[:, pl.ds(CP, CP)], sw_send)
    await_bytes(rets, rt_send)
    await_bytes(outs.at[pl.ds(0, 2 * (NY - 1))], out_send)
    await_bytes(back.at[pl.ds(0, group - 1)], pb_send)


def body(NX, NY, NZ, grad_out, probs, expert_ids, slot_ids, w_down, hidden):
    T, D = grad_out.shape
    ff, BL = w_down.shape[1:]
    cells = hidden.shape[2]
    group = NX * NY
    per = cells // group
    NB, NI = NY // 2, NY // 4
    C0 = NX * per
    CP = -(-(C0 + NX) // 16) * 16
    cell = np.arange(cells)
    src, s = cell // per, cell % per
    n, l = src // NY, src % NY
    tab = np.zeros((8, cells), np.int32)
    tab[0] = l * CP + n * per + s
    tab[1] = src
    tab[2] = s
    tab[3] = l * 16 + C0 % 16 + n
    vm = pl.BlockSpec(memory_space=pltpu.VMEM)
    anym = pl.BlockSpec(memory_space=pl.ANY)
    V, DMA = pltpu.VMEM, pltpu.SemaphoreType.DMA
    dh, dpr = pl.pallas_call(
        functools.partial(kernel, NX, NY, NZ, per, BL),
        out_shape=(jax.ShapeDtypeStruct((ff // NY, cells), BF), jax.ShapeDtypeStruct((8, T), F32)),
        in_specs=[anym, vm, vm, vm, vm, anym, anym],
        out_specs=(vm, vm),
        scratch_shapes=[
            V((T, D), BF), V((ff, BL), BF), V((ff // NY, cells), BF),
            V((NX - 1, NY, 48, BL), BF), V((NY, NX, 48, BL), BF),
            V((NB, CP, BL), BF), V((NB, 2 * CP, BL), BF),
            V((ROUNDS * 2 * NZ, NB - 1, NI * 128 // NZ, BL), BF),
            V((2 * ROUNDS, CP, NI * 128), BF), V((2 * ROUNDS, CP, NI * 128), BF),
            V((2, CP, NI * 128), F32), V((2 * ROUNDS * NI, CP, 128), BF),
            V((2 * NY, CP, 128), BF), V((CP, 128), BF), V((NY * CP, cells), BF),
            V((group, 8, 128), F32), V((group, 8, 128), F32),
            DMA((3,)), DMA, DMA((ROUNDS,)), DMA((ROUNDS * NZ,)), DMA((ROUNDS,)), DMA, DMA((2,)),
            DMA, DMA, DMA, DMA((2 * ROUNDS,)), DMA, DMA((2,)), DMA, DMA,
        ],
        compiler_params=pltpu.CompilerParams(
            collective_id=0, has_side_effects=True, vmem_limit_bytes=58 * 1024 * 1024),
        cost_estimate=pl.CostEstimate(flops=2 * ff * cells * BL, bytes_accessed=8 << 20,
                                      transcendentals=0),
    )(grad_out, expert_ids.reshape(1, T), slot_ids.reshape(1, T), probs.reshape(1, T),
      jnp.asarray(tab), w_down[0], hidden[0])
    return dh[None], dpr[0]


def solution(mesh):
    NX, NY, NZ = mesh.shape["node"], mesh.shape["local"], mesh.shape["dp"] // 2
    return jax.shard_map(
        functools.partial(body, NX, NY, NZ),
        mesh=mesh,
        in_specs=(
            P(("dp", "node", "local"), None),
            P(("dp", "node", "local")),
            P(("dp", "node", "local")),
            P(("dp", "node", "local")),
            P("node", None, "local"),
            P(("dp", "node"), "local", None),
        ),
        out_specs=(P(("dp", "node"), "local", None), P(("dp", "node", "local"))),
        check_vma=False,
    )
```

```python
import contextlib
import functools

import jax
import jax.numpy as jnp
from jax import lax
from jax.experimental import pallas as pl
from jax.experimental.pallas import tpu as pltpu
from jax.sharding import PartitionSpec as P

MESH = pl.DeviceIdType.MESH
BF = jnp.bfloat16
F32 = jnp.float32
ROUNDS = 4
STAGGER = 2
DIRECT = (2, 2, 2, 2)
COMPACT = (4, 6)
NT = (((1,), (1,)), ((), ()))


def stage(_):
    return contextlib.nullcontext()


def kernel(NX, NY, NZ, per, BL, grad_h, eid_ref, sid_ref, prob_ref, w_h, hid_h,
           dh_ref, dp_ref,
           grad_v, w_v, hid_v, sendx, rx, swap, tok, wbuf, rets, retr, own, outs, res, wpad, perm,
           wcol, zacc, msgs, back,
           load_sem, yf_send, ring_send, ring_sem, sib_sem, xs_sem, xr_sem, sw_send, sw_recv,
           rt_send, rt_recv, out_send, out_recv, pb_send, pb_recv):
    NB = NY // 2
    NI = NY // 4
    CR = NI * 128 // NZ
    SL = 48
    C0 = NX * per
    CP = -(-(C0 + NX) // 16) * 16
    CA = -(-(CP // 2) // 16) * 16
    CELLS = NX * NY * per

    x = lax.axis_index("node")
    y = lax.axis_index("local")
    dp = lax.axis_index("dp")
    z = lax.div(dp, 2)
    k = lax.rem(dp, 2)
    par = lax.rem(y, 2)
    sib = {"dp": dp + 1 - 2 * k}
    z_up = {"dp": lax.rem(z + 1, NZ) * 2 + k}
    z_dn = {"dp": lax.rem(z + NZ - 1, NZ) * 2 + k}
    y_up = {"local": lax.rem(y + 1, NY)}
    y_dn = {"local": lax.rem(y + NY - 1, NY)}

    def remote(src, dst, ss, rs, dev):
        pltpu.make_async_remote_copy(src_ref=src, dst_ref=dst, send_sem=ss, recv_sem=rs,
                                     device_id=dev, device_id_type=MESH).start()

    def await_bytes(ref, sem):
        pltpu.make_async_copy(ref, ref, sem).wait()

    g_copy = pltpu.make_async_copy(grad_h, grad_v, load_sem.at[0])
    g_copy.start()
    w_copy = pltpu.make_async_copy(w_h, w_v, load_sem.at[1])
    w_copy.start()
    h_copy = pltpu.make_async_copy(hid_h, hid_v, load_sem.at[2])
    h_copy.start()

    bar = pltpu.get_barrier_semaphore()
    group = NX * NY
    mine = x * NY + y

    def greet(i, _):
        p = lax.rem(mine + i, group)
        pl.semaphore_signal(bar, inc=1, device_id={"node": lax.div(p, NY), "local": lax.rem(p, NY)},
                            device_id_type=MESH)
        return 0

    for dev in (z_up, z_dn, sib):
        pl.semaphore_signal(bar, inc=1, device_id=dev, device_id_type=MESH)
    lax.fori_loop(1, group, greet, 0)
    pl.semaphore_wait(bar, group - 1 + 3)

    def share(r, plane):
        at = plane * CR
        row = (NB * k + 2 * lax.div(at, 128) + r % 2) * 256 + 128 * (r // 2) + lax.rem(at, 128)
        row = pl.multiple_of(row, 16)
        for j in range(1, NB):
            remote(w_h.at[pl.ds(row, CR)], wbuf.at[(r * 2 + k) * NZ + plane, j - 1], yf_send,
                   ring_sem.at[(r * NZ + plane) * (NB - 1) + j - 1],
                   {"local": lax.rem(y + NY - 2 * j, NY)})

    count = [min(DIRECT[r], NZ - 1) for r in range(ROUNDS)]
    up = [(NZ - 1 - count[r] + (r % 2 == 0)) // 2 for r in range(ROUNDS)]
    down = [NZ - 1 - count[r] - up[r] for r in range(ROUNDS)]
    last = [max(up[r], down[r]) for r in range(ROUNDS)]

    def direct(r):
        return [lax.rem(z + down[r] + 1 + i, NZ) for i in range(count[r])]

    share(0, z)
    share(1, z)

    g_copy.wait()
    eid, sid = eid_ref[...], sid_ref[...]
    prow = jnp.broadcast_to(prob_ref[...], (16, prob_ref.shape[1])).astype(BF)
    T = eid.shape[1]
    rows_sl = lax.broadcasted_iota(jnp.int32, (SL, T), 0)
    rows_w = lax.broadcasted_iota(jnp.int32, (128, T), 0)
    rows_sl2 = lax.broadcasted_iota(jnp.int32, (SL, 128), 0)
    hot, wts = [], []
    for i in range(NX):
        e = lax.rem(x + i, NX)
        hot.append(jnp.where((eid == e) & (sid == rows_sl), 1.0, 0.0))
        hot_w = jnp.where((eid == e) & (sid == rows_w), 1.0, 0.0).astype(BF)
        wt = lax.dot_general(prow, hot_w, NT, preferred_element_type=F32)[0:1]
        wts.append(jnp.where(rows_sl2 == per, jnp.broadcast_to(wt, (SL, 128)), 0.0))
    hot = jnp.concatenate(hot, axis=0).astype(BF)
    wts = jnp.concatenate(wts, axis=0)
    def pack(ph):
        pp = 1 - par if ph == 0 else par
        for jj in range(NB):
            b = 2 * jj + pp
            lanes = pl.ds(pl.multiple_of(b * BL, 128), BL)
            val = jnp.dot(hot, grad_v[:, lanes], preferred_element_type=F32)
            first = (val[:, 0:128] + wts).astype(BF)
            val = val.astype(BF)
            pj = pp * NB + jj
            for i in range(NX):
                cut = slice(SL * i, SL * (i + 1))
                if i == 0:
                    rx[pj, x] = val[cut]
                    rx[pj, x, :, 0:128] = first[cut]
                else:
                    sendx[i - 1, pj] = val[cut]
                    sendx[i - 1, pj, :, 0:128] = first[cut]
        for i in range(1, NX):
            remote(sendx.at[i - 1, pl.ds(pp * NB, NB)], rx.at[pl.ds(pp * NB, NB), x], xs_sem,
                   xr_sem.at[ph], {"node": lax.rem(x + i, NX)})

    def ring(r, d):
        base = (r * 2 + k) * NZ

        def chunk(src, j):
            await_bytes(wbuf.at[base + src, j], ring_sem.at[(r * NZ + src) * (NB - 1) + j])

        def pass_on(src, j, dev):
            remote(wbuf.at[base + src, j], wbuf.at[base + src, j], ring_send.at[r],
                   ring_sem.at[(r * NZ + src) * (NB - 1) + j], dev)

        def to_sibling(src):
            remote(wbuf.at[base + src], wbuf.at[base + src], ring_send.at[r], sib_sem.at[r], sib)

        moves = []
        if d == 0:
            moves.append((z, [z_up] * (up[r] > 0) + [z_dn] * (down[r] > 0)))
        if 0 < d <= up[r]:
            moves.append((lax.rem(z + NZ - d, NZ), [z_up] if d < up[r] else []))
        if 0 < d <= down[r]:
            moves.append((lax.rem(z + d, NZ), [z_dn] if d < down[r] else []))
        if d == last[r]:
            moves.extend((plane, []) for plane in direct(r))
        for j in range(NB - 1):
            for src, devs in moves:
                chunk(src, j)
                for dev in devs:
                    pass_on(src, j, dev)
        for src, _ in moves:
            to_sibling(src)

    def compact(ph):
        q = lax.broadcasted_iota(jnp.int32, (CP, NX * SL), 0)
        c = lax.broadcasted_iota(jnp.int32, (CP, NX * SL), 1)
        keep = q < 0
        for n in range(NX):
            keep = keep | ((q >= per * n) & (q < per * (n + 1)) & (c - SL * n == q - per * n))
            keep = keep | ((q == C0 + n) & (c == SL * n + per))
        pick = jnp.where(keep, 1.0, 0.0).astype(BF)
        await_bytes(sendx.at[:, pl.ds(0, NB)], xr_sem.at[ph])
        pp = 1 - par if ph == 0 else par
        for j in range(NB):
            jj = j if ph == 0 else lax.div(lax.rem(y + 2 * j, NY), 2)
            got = rx[pp * NB + jj].reshape(NX * SL, BL)
            val = jnp.dot(pick, got, preferred_element_type=F32).astype(BF)
            if ph == 0:
                swap[jj] = val
            else:
                tok[j, 0:CP] = val
                if j == 0:
                    wpad[...] = val[:, 0:128]
        if ph == 0:
            for j in range(NB):
                lo = lax.div(lax.rem(y + NY - 1 + 2 * j, NY), 2)
                hi = lax.div(lax.rem(y + 1 + 2 * j, NY), 2)
                remote(swap.at[lo, pl.ds(0, CA)], tok.at[j, pl.ds(CP, CA)], sw_send, sw_recv, y_dn)
                remote(swap.at[hi, pl.ds(CA, CP - CA)], tok.at[j, pl.ds(CP + CA, CP - CA)],
                       sw_send, sw_recv, y_up)

    def compute(r, step):
        if step == 1:
            await_bytes(wbuf.at[pl.ds((r * 2 + 1 - k) * NZ, NZ)], sib_sem.at[r])
        kk = k if step == 0 else 1 - k
        own_w = [w_v[pl.ds(pl.multiple_of(
            (NB * kk + 2 * i + r % 2) * 256 + 128 * (r // 2), 128), 128), :] for i in range(NI)]
        own_w = jnp.concatenate(own_w, axis=0) if NI > 1 else own_w[0]
        acc = lax.dot_general(tok[0], own_w, NT, preferred_element_type=F32)
        for j in range(1, NB):
            wj = wbuf[pl.ds((r * 2 + kk) * NZ, NZ), j - 1].reshape(NI * 128, BL)
            acc = acc + lax.dot_general(tok[j], wj, NT, preferred_element_type=F32)
        m = r * 2 + step
        rets[m] = acc[CP:2 * CP].astype(BF)
        remote(rets.at[m, pl.ds(0, CA)], retr.at[m, pl.ds(0, CA)], rt_send, rt_recv.at[m], y_up)
        remote(rets.at[m, pl.ds(CA, CP - CA)], retr.at[m, pl.ds(CA, CP - CA)], rt_send,
               rt_recv.at[m], y_dn)
        own[step] = acc[0:CP]

    def finish(r, step):
        h = r // 2
        kk = k if step == 0 else 1 - k
        rows = lax.broadcasted_iota(jnp.int32, (CP, 128), 0)
        m = r * 2 + step
        await_bytes(retr.at[m], rt_recv.at[m])
        for i in range(NI):
            cut = slice(128 * i, 128 * (i + 1))
            val = own[step, :, cut] + retr[m, :, cut].astype(F32)
            val = jnp.where(rows >= C0, wpad[...].astype(F32), val).astype(BF)
            dest = NB * kk + 2 * i + r % 2
            slot = m * NI + i
            outs[slot] = val

            @pl.when(y != dest)
            def _():
                remote(outs.at[slot], res.at[h * NY + y], out_send, out_recv.at[h],
                       {"local": dest})

            @pl.when(y == dest)
            def _():
                res[h * NY + dest] = val

    def cell_parts(rows, lanes, dim):
        c = lax.broadcasted_iota(jnp.int32, (rows, lanes), dim).astype(F32)
        src = jnp.floor((c + 0.5) / per)
        n = jnp.floor((src + 0.5) / NY)
        return (v.astype(jnp.int32) for v in (src, c - per * src, n, src - NY * n))

    def build_perm():
        _, s, n, l = cell_parts(CELLS, 128, 0)
        at = l * CP + n * per + s
        for lo in range(0, NY * CP, 128):
            width = min(128, NY * CP - lo)
            q = lax.broadcasted_iota(jnp.int32, (CELLS, width), 1) + lo
            perm[:, lo:lo + width] = jnp.where(q == at[:, :width], 1.0, 0.0).astype(BF)

    def tail(h):
        await_bytes(res.at[pl.ds(0, NY - 1)], out_recv.at[h])
        got = res[h * NY:(h + 1) * NY]
        raw = jnp.dot(perm[...], got.reshape(NY * CP, 128), preferred_element_type=F32)
        if h == 0:
            _, s, n, l = cell_parts(CELLS, 128, 0)
            last = C0 // 16 * 16
            sheet = got[:, last:last + 16, :].reshape(NY * 16, 128)
            at = (l * 16 + C0 % 16 + n)[:, :NY * 16]
            q = lax.broadcasted_iota(jnp.int32, (CELLS, NY * 16), 1)
            wide = jnp.dot(jnp.where(q == at, 1.0, 0.0).astype(BF), sheet, preferred_element_type=F32)
            lane = lax.broadcasted_iota(jnp.int32, (CELLS, 128), 1)
            one = jnp.sum(jnp.where(lane == s, wide, 0.0), axis=1, keepdims=True)
            wcol[...] = jnp.broadcast_to(one, (CELLS, 128))
        cut = slice(128 * h, 128 * (h + 1))
        dh_ref[:, cut] = (raw * wcol[...]).astype(BF)
        part = hid_v[:, cut].astype(F32) * raw
        if h == 0:
            zacc[...] = part
        else:
            zacc[...] = zacc[...] + part

    with stage("pack0"):
        pack(0)
    done = [last[r] + STAGGER * r for r in range(ROUNDS)]
    for t in range(max(done) + 1):
        for r in range(ROUNDS):
            if 0 <= t - STAGGER * r <= last[r]:
                with stage(f"ring{r}_{t - STAGGER * r}"):
                    ring(r, t - STAGGER * r)
        if t == 0:
            share(2, z)
            share(3, z)
            with stage("pack1"):
                pack(1)
            for r in range(ROUNDS):
                share(r, direct(r)[0])
        if t == min(1, last[0] - 1):
            with stage("perm"):
                build_perm()
                w_copy.wait()
                h_copy.wait()
            for r in range(ROUNDS):
                for plane in direct(r)[1:]:
                    share(r, plane)
        if t == min(COMPACT[0], last[0]):
            with stage("compact0"):
                compact(0)
        if t == min(COMPACT[1], last[0]):
            with stage("compact1"):
                compact(1)
        if t == done[0]:
            with stage("swapwait"):
                await_bytes(tok.at[:, pl.ds(CP, CP)], sw_recv)
        for r in range(ROUNDS):
            if t == done[r] + 1:
                with stage(f"finish{r}"):
                    finish(r, 0)
                    finish(r, 1)
        for r in range(ROUNDS):
            if t == done[r]:
                with stage(f"compute{r}"):
                    compute(r, 0)
                    compute(r, 1)
    finish(ROUNDS - 1, 0)
    with stage("tail0"):
        tail(0)
    finish(ROUNDS - 1, 1)
    with stage("tail1"):
        tail(1)

    _, s, _, _ = cell_parts(CELLS, 128, 0)
    lane = lax.broadcasted_iota(jnp.int32, (CELLS, 128), 1)
    spread = jnp.where(lane == s, jnp.sum(zacc[...], axis=1, keepdims=True), 0.0)
    src, _, _, _ = cell_parts(group, CELLS, 1)
    pick = jnp.where(src == lax.broadcasted_iota(jnp.int32, (group, CELLS), 0), 1.0, 0.0)
    rows = jnp.dot(pick, spread, preferred_element_type=F32, precision=lax.Precision.HIGHEST)
    msgs[...] = jnp.broadcast_to(rows[:, None, :], (group, 8, 128))
    back[mine] = msgs[mine]

    def give(i, _):
        p = lax.rem(mine + i, group)
        remote(msgs.at[p], back.at[mine], pb_send, pb_recv,
               {"node": lax.div(p, NY), "local": lax.rem(p, NY)})
        return 0

    lax.fori_loop(1, group, give, 0)
    await_bytes(back.at[pl.ds(0, group - 1)], pb_recv)
    sums = jnp.concatenate(
        [jnp.sum(back[e * NY:(e + 1) * NY], axis=0)[0:1] for e in range(NX)]
        + [jnp.zeros((8 - NX, 128), F32)], axis=0)
    slot_hot = jnp.where(sid == rows_w, 1.0, 0.0)
    got = jnp.dot(sums, slot_hot, preferred_element_type=F32, precision=lax.Precision.HIGHEST)
    total = jnp.sum(jnp.where(eid == lax.broadcasted_iota(jnp.int32, (8, T), 0), got, 0.0),
                    axis=0, keepdims=True)
    dp_ref[...] = total

    await_bytes(wbuf.at[pl.ds(0, ROUNDS + sum(count))], yf_send)
    for r in range(ROUNDS):
        await_bytes(wbuf.at[pl.ds(0, NZ + up[r] + down[r])], ring_send.at[r])
    await_bytes(sendx, xs_sem)
    await_bytes(tok.at[:, pl.ds(CP, CP)], sw_send)
    await_bytes(rets, rt_send)
    await_bytes(outs.at[pl.ds(0, 2 * (NY - 1))], out_send)
    await_bytes(back.at[pl.ds(0, group - 1)], pb_send)


def body(NX, NY, NZ, grad_out, probs, expert_ids, slot_ids, w_down, hidden):
    T, D = grad_out.shape
    ff, BL = w_down.shape[1:]
    cells = hidden.shape[2]
    group = NX * NY
    per = cells // group
    NB, NI = NY // 2, NY // 4
    C0 = NX * per
    CP = -(-(C0 + NX) // 16) * 16
    vm = pl.BlockSpec(memory_space=pltpu.VMEM)
    anym = pl.BlockSpec(memory_space=pl.ANY)
    V, DMA = pltpu.VMEM, pltpu.SemaphoreType.DMA
    dh, dpr = pl.pallas_call(
        functools.partial(kernel, NX, NY, NZ, per, BL),
        out_shape=(jax.ShapeDtypeStruct((cells, ff // NY), BF), jax.ShapeDtypeStruct((1, T), F32)),
        in_specs=[anym, vm, vm, vm, anym, anym],
        out_specs=(vm, vm),
        scratch_shapes=[
            V((T, D), BF), V((ff, BL), BF), V((cells, ff // NY), BF),
            V((NX - 1, NY, 48, BL), BF), V((NY, NX, 48, BL), BF),
            V((NB, CP, BL), BF), V((NB, 2 * CP, BL), BF),
            V((ROUNDS * 2 * NZ, NB - 1, NI * 128 // NZ, BL), BF),
            V((2 * ROUNDS, CP, NI * 128), BF), V((2 * ROUNDS, CP, NI * 128), BF),
            V((2, CP, NI * 128), F32), V((2 * ROUNDS * NI, CP, 128), BF),
            V((2 * NY, CP, 128), BF), V((CP, 128), BF), V((cells, NY * CP), BF),
            V((cells, 128), F32), V((cells, 128), F32),
            V((group, 8, 128), F32), V((group, 8, 128), F32),
            DMA((3,)), DMA, DMA((ROUNDS,)), DMA((ROUNDS * NZ * (NB - 1),)), DMA((ROUNDS,)), DMA, DMA((2,)),
            DMA, DMA, DMA, DMA((2 * ROUNDS,)), DMA, DMA((2,)), DMA, DMA,
        ],
        compiler_params=pltpu.CompilerParams(
            collective_id=0, has_side_effects=True, vmem_limit_bytes=58 * 1024 * 1024),
        cost_estimate=pl.CostEstimate(flops=2 * ff * cells * BL, bytes_accessed=8 << 20,
                                      transcendentals=0),
    )(grad_out, expert_ids.reshape(1, T), slot_ids.reshape(1, T), probs.reshape(1, T),
      w_down[0], hidden[0].T)
    return dh.T[None], dpr[0]


def solution(mesh):
    NX, NY, NZ = mesh.shape["node"], mesh.shape["local"], mesh.shape["dp"] // 2
    return jax.shard_map(
        functools.partial(body, NX, NY, NZ),
        mesh=mesh,
        in_specs=(
            P(("dp", "node", "local"), None),
            P(("dp", "node", "local")),
            P(("dp", "node", "local")),
            P(("dp", "node", "local")),
            P("node", None, "local"),
            P(("dp", "node"), "local", None),
        ),
        out_specs=(P(("dp", "node"), "local", None), P(("dp", "node", "local"))),
        check_vma=False,
    )
```

```python
import contextlib
import functools

import jax
import jax.numpy as jnp
from jax import lax
from jax.experimental import pallas as pl
from jax.experimental.pallas import tpu as pltpu
from jax.sharding import PartitionSpec as P

MESH = pl.DeviceIdType.MESH
BF = jnp.bfloat16
F32 = jnp.float32
ROUNDS = 4
START = (0, 1, 3, 5)
DIRECT = (2, 2, 2, 2)
COMPACT = (4, 6)
NT = (((1,), (1,)), ((), ()))


def stage(_):
    return contextlib.nullcontext()


def kernel(NX, NY, NZ, per, BL, grad_h, eid_ref, sid_ref, prob_ref, w_h, hid_h,
           dh_ref, dp_ref,
           grad_v, w_v, hid_v, sendx, rx, swap, tok, wbuf, rets, retr, own, outs, res, wpad, perm,
           wcol, zacc, msgs, back,
           load_sem, yf_send, ring_send, ring_sem, sib_sem, xs_sem, xr_sem, sw_send, sw_recv,
           rt_send, rt_recv, out_send, out_recv, pb_send, pb_recv):
    NB = NY // 2
    NI = NY // 4
    CR = NI * 128 // NZ
    SL = 48
    C0 = NX * per
    CP = -(-(C0 + NX) // 16) * 16
    CA = -(-(CP // 2) // 16) * 16
    CELLS = NX * NY * per

    x = lax.axis_index("node")
    y = lax.axis_index("local")
    dp = lax.axis_index("dp")
    z = lax.div(dp, 2)
    k = lax.rem(dp, 2)
    par = lax.rem(y, 2)
    sib = {"dp": dp + 1 - 2 * k}
    z_up = {"dp": lax.rem(z + 1, NZ) * 2 + k}
    z_dn = {"dp": lax.rem(z + NZ - 1, NZ) * 2 + k}
    y_up = {"local": lax.rem(y + 1, NY)}
    y_dn = {"local": lax.rem(y + NY - 1, NY)}

    def remote(src, dst, ss, rs, dev):
        pltpu.make_async_remote_copy(src_ref=src, dst_ref=dst, send_sem=ss, recv_sem=rs,
                                     device_id=dev, device_id_type=MESH).start()

    def await_bytes(ref, sem):
        pltpu.make_async_copy(ref, ref, sem).wait()

    g_copy = pltpu.make_async_copy(grad_h, grad_v, load_sem.at[0])
    g_copy.start()
    w_copy = pltpu.make_async_copy(w_h, w_v, load_sem.at[1])
    w_copy.start()
    h_copy = pltpu.make_async_copy(hid_h, hid_v, load_sem.at[2])
    h_copy.start()

    bar = pltpu.get_barrier_semaphore()
    group = NX * NY
    mine = x * NY + y

    def greet(i, _):
        p = lax.rem(mine + i, group)
        pl.semaphore_signal(bar, inc=1, device_id={"node": lax.div(p, NY), "local": lax.rem(p, NY)},
                            device_id_type=MESH)
        return 0

    for dev in (z_up, z_dn, sib):
        pl.semaphore_signal(bar, inc=1, device_id=dev, device_id_type=MESH)
    for i in range(1, group):
        greet(i, 0)
    pl.semaphore_wait(bar, group - 1 + 3)

    def share(r, plane):
        at = plane * CR
        row = (NB * k + 2 * lax.div(at, 128) + r % 2) * 256 + 128 * (r // 2) + lax.rem(at, 128)
        row = pl.multiple_of(row, 16)
        for j in range(1, NB):
            remote(w_h.at[pl.ds(row, CR)], wbuf.at[(r * 2 + k) * NZ + plane, j - 1], yf_send,
                   ring_sem.at[(r * NZ + plane) * (NB - 1) + j - 1],
                   {"local": lax.rem(y + NY - 2 * j, NY)})

    count = [min(DIRECT[r], NZ - 1) for r in range(ROUNDS)]
    up = [(NZ - 1 - count[r] + (r % 2 == 0)) // 2 for r in range(ROUNDS)]
    down = [NZ - 1 - count[r] - up[r] for r in range(ROUNDS)]
    last = [max(up[r], down[r]) for r in range(ROUNDS)]

    def direct(r):
        return [lax.rem(z + down[r] + 1 + i, NZ) for i in range(count[r])]

    share(0, z)
    share(1, z)

    g_copy.wait()
    eid, sid = eid_ref[...], sid_ref[...]
    prow = jnp.broadcast_to(prob_ref[...], (16, prob_ref.shape[1])).astype(BF)
    T = eid.shape[1]
    rows_sl = lax.broadcasted_iota(jnp.int32, (SL, T), 0)
    rows_w = lax.broadcasted_iota(jnp.int32, (128, T), 0)
    rows_sl2 = lax.broadcasted_iota(jnp.int32, (SL, 128), 0)
    hot, wts = [], []
    for i in range(NX):
        e = lax.rem(x + i, NX)
        hot.append(jnp.where((eid == e) & (sid == rows_sl), 1.0, 0.0))
        hot_w = jnp.where((eid == e) & (sid == rows_w), 1.0, 0.0).astype(BF)
        wt = lax.dot_general(prow, hot_w, NT, preferred_element_type=F32)[0:1]
        wts.append(jnp.where(rows_sl2 == per, jnp.broadcast_to(wt, (SL, 128)), 0.0))
    hot = jnp.concatenate(hot, axis=0).astype(BF)
    wts = jnp.concatenate(wts, axis=0)
    def pack(ph):
        pp = 1 - par if ph == 0 else par
        for jj in range(NB):
            b = 2 * jj + pp
            lanes = pl.ds(pl.multiple_of(b * BL, 128), BL)
            val = jnp.dot(hot, grad_v[:, lanes], preferred_element_type=F32)
            first = (val[:, 0:128] + wts).astype(BF)
            val = val.astype(BF)
            pj = pp * NB + jj
            for i in range(NX):
                cut = slice(SL * i, SL * (i + 1))
                if i == 0:
                    rx[pj, x] = val[cut]
                    rx[pj, x, :, 0:128] = first[cut]
                else:
                    sendx[i - 1, pj] = val[cut]
                    sendx[i - 1, pj, :, 0:128] = first[cut]
        for i in range(1, NX):
            remote(sendx.at[i - 1, pl.ds(pp * NB, NB)], rx.at[pl.ds(pp * NB, NB), x], xs_sem,
                   xr_sem.at[ph], {"node": lax.rem(x + i, NX)})

    def ring(r, d):
        base = (r * 2 + k) * NZ

        def chunk(src, j):
            await_bytes(wbuf.at[base + src, j], ring_sem.at[(r * NZ + src) * (NB - 1) + j])

        def pass_on(src, j, dev):
            remote(wbuf.at[base + src, j], wbuf.at[base + src, j], ring_send.at[r],
                   ring_sem.at[(r * NZ + src) * (NB - 1) + j], dev)

        def to_sibling(src):
            remote(wbuf.at[base + src], wbuf.at[base + src], ring_send.at[r], sib_sem.at[r], sib)

        moves = []
        if d == 0:
            moves.append((z, [z_up] * (up[r] > 0) + [z_dn] * (down[r] > 0)))
        if 0 < d <= up[r]:
            moves.append((lax.rem(z + NZ - d, NZ), [z_up] if d < up[r] else []))
        if 0 < d <= down[r]:
            moves.append((lax.rem(z + d, NZ), [z_dn] if d < down[r] else []))
        if d == last[r]:
            moves.extend((plane, []) for plane in direct(r))
        for j in range(NB - 1):
            for src, devs in moves:
                chunk(src, j)
                for dev in devs:
                    pass_on(src, j, dev)
        for src, _ in moves:
            to_sibling(src)

    def compact(ph):
        q = lax.broadcasted_iota(jnp.int32, (CP, NX * SL), 0)
        c = lax.broadcasted_iota(jnp.int32, (CP, NX * SL), 1)
        keep = q < 0
        for n in range(NX):
            keep = keep | ((q >= per * n) & (q < per * (n + 1)) & (c - SL * n == q - per * n))
            keep = keep | ((q == C0 + n) & (c == SL * n + per))
        pick = jnp.where(keep, 1.0, 0.0).astype(BF)
        await_bytes(sendx.at[:, pl.ds(0, NB)], xr_sem.at[ph])
        pp = 1 - par if ph == 0 else par
        for j in range(NB):
            jj = j if ph == 0 else lax.div(lax.rem(y + 2 * j, NY), 2)
            got = rx[pp * NB + jj].reshape(NX * SL, BL)
            val = jnp.dot(pick, got, preferred_element_type=F32).astype(BF)
            if ph == 0:
                swap[jj] = val
            else:
                tok[j, 0:CP] = val
                if j == 0:
                    wpad[...] = val[:, 0:128]
        if ph == 0:
            for j in range(NB):
                lo = lax.div(lax.rem(y + NY - 1 + 2 * j, NY), 2)
                hi = lax.div(lax.rem(y + 1 + 2 * j, NY), 2)
                remote(swap.at[lo, pl.ds(0, CA)], tok.at[j, pl.ds(CP, CA)], sw_send, sw_recv, y_dn)
                remote(swap.at[hi, pl.ds(CA, CP - CA)], tok.at[j, pl.ds(CP + CA, CP - CA)],
                       sw_send, sw_recv, y_up)

    def compute(r, step):
        if step == 1:
            await_bytes(wbuf.at[pl.ds((r * 2 + 1 - k) * NZ, NZ)], sib_sem.at[r])
        kk = k if step == 0 else 1 - k
        own_w = [w_v[pl.ds(pl.multiple_of(
            (NB * kk + 2 * i + r % 2) * 256 + 128 * (r // 2), 128), 128), :] for i in range(NI)]
        own_w = jnp.concatenate(own_w, axis=0) if NI > 1 else own_w[0]
        acc = lax.dot_general(tok[0], own_w, NT, preferred_element_type=F32)
        for j in range(1, NB):
            wj = wbuf[pl.ds((r * 2 + kk) * NZ, NZ), j - 1].reshape(NI * 128, BL)
            acc = acc + lax.dot_general(tok[j], wj, NT, preferred_element_type=F32)
        m = r * 2 + step
        rets[m] = acc[CP:2 * CP].astype(BF)
        remote(rets.at[m, pl.ds(0, CA)], retr.at[m, pl.ds(0, CA)], rt_send, rt_recv.at[m], y_up)
        remote(rets.at[m, pl.ds(CA, CP - CA)], retr.at[m, pl.ds(CA, CP - CA)], rt_send,
               rt_recv.at[m], y_dn)
        own[step] = acc[0:CP]

    def finish(r, step):
        h = r // 2
        kk = k if step == 0 else 1 - k
        rows = lax.broadcasted_iota(jnp.int32, (CP, 128), 0)
        m = r * 2 + step
        await_bytes(retr.at[m], rt_recv.at[m])
        for i in range(NI):
            cut = slice(128 * i, 128 * (i + 1))
            val = own[step, :, cut] + retr[m, :, cut].astype(F32)
            val = jnp.where(rows >= C0, wpad[...].astype(F32), val).astype(BF)
            dest = NB * kk + 2 * i + r % 2
            slot = m * NI + i
            outs[slot] = val

            @pl.when(y != dest)
            def _():
                remote(outs.at[slot], res.at[h * NY + y], out_send, out_recv.at[h],
                       {"local": dest})

            @pl.when(y == dest)
            def _():
                res[h * NY + dest] = val

    def cell_parts(rows, lanes, dim):
        c = lax.broadcasted_iota(jnp.int32, (rows, lanes), dim).astype(F32)
        src = jnp.floor((c + 0.5) / per)
        n = jnp.floor((src + 0.5) / NY)
        return (v.astype(jnp.int32) for v in (src, c - per * src, n, src - NY * n))

    def build_perm():
        _, s, n, l = cell_parts(CELLS, 128, 0)
        at = l * CP + n * per + s
        for lo in range(0, NY * CP, 128):
            width = min(128, NY * CP - lo)
            q = lax.broadcasted_iota(jnp.int32, (CELLS, width), 1) + lo
            perm[:, lo:lo + width] = jnp.where(q == at[:, :width], 1.0, 0.0).astype(BF)

    def tail(h):
        await_bytes(res.at[pl.ds(0, NY - 1)], out_recv.at[h])
        got = res[h * NY:(h + 1) * NY]
        raw = jnp.dot(perm[...], got.reshape(NY * CP, 128), preferred_element_type=F32)
        if h == 0:
            _, s, n, l = cell_parts(CELLS, 128, 0)
            last = C0 // 16 * 16
            sheet = got[:, last:last + 16, :].reshape(NY * 16, 128)
            at = (l * 16 + C0 % 16 + n)[:, :NY * 16]
            q = lax.broadcasted_iota(jnp.int32, (CELLS, NY * 16), 1)
            wide = jnp.dot(jnp.where(q == at, 1.0, 0.0).astype(BF), sheet, preferred_element_type=F32)
            lane = lax.broadcasted_iota(jnp.int32, (CELLS, 128), 1)
            one = jnp.sum(jnp.where(lane == s, wide, 0.0), axis=1, keepdims=True)
            wcol[...] = jnp.broadcast_to(one, (CELLS, 128))
        cut = slice(128 * h, 128 * (h + 1))
        dh_ref[:, cut] = (raw * wcol[...]).astype(BF)
        part = hid_v[:, cut].astype(F32) * raw
        if h == 0:
            zacc[...] = part
        else:
            zacc[...] = zacc[...] + part

    with stage("pack0"):
        pack(0)
    done = [last[r] + START[r] for r in range(ROUNDS)]
    for t in range(max(done) + 1):
        for r in range(ROUNDS):
            if 0 <= t - START[r] <= last[r]:
                with stage(f"ring{r}_{t - START[r]}"):
                    ring(r, t - START[r])
        if t == 0:
            share(2, z)
            share(3, z)
            for r in range(ROUNDS):
                share(r, direct(r)[0])
        if t == min(2, last[0] - 1):
            with stage("pack1"):
                pack(1)
        if t == min(5, last[0] - 1):
            with stage("perm"):
                build_perm()
                w_copy.wait()
                h_copy.wait()
        if t == min(1, last[0] - 1):
            for r in range(ROUNDS):
                for plane in direct(r)[1:]:
                    share(r, plane)
        if t == min(COMPACT[0], last[0]):
            with stage("compact0"):
                compact(0)
        if t == min(COMPACT[1], last[0]):
            with stage("compact1"):
                compact(1)
        if t == done[0]:
            with stage("swapwait"):
                await_bytes(tok.at[:, pl.ds(CP, CP)], sw_recv)
        for r in range(ROUNDS):
            if t == done[r] + 1:
                with stage(f"finish{r}"):
                    finish(r, 0)
                    finish(r, 1)
        for r in range(ROUNDS):
            if t == done[r]:
                with stage(f"compute{r}"):
                    compute(r, 0)
                    compute(r, 1)
    finish(ROUNDS - 1, 0)
    with stage("tail0"):
        tail(0)
    finish(ROUNDS - 1, 1)
    with stage("tail1"):
        tail(1)

    _, s, _, _ = cell_parts(CELLS, 128, 0)
    lane = lax.broadcasted_iota(jnp.int32, (CELLS, 128), 1)
    spread = jnp.where(lane == s, jnp.sum(zacc[...], axis=1, keepdims=True), 0.0)
    src, _, _, _ = cell_parts(group, CELLS, 1)
    pick = jnp.where(src == lax.broadcasted_iota(jnp.int32, (group, CELLS), 0), 1.0, 0.0)
    rows = jnp.dot(pick, spread, preferred_element_type=F32, precision=lax.Precision.HIGHEST)
    msgs[...] = jnp.broadcast_to(rows[:, None, :], (group, 8, 128))
    back[mine] = msgs[mine]

    def give(i, _):
        p = lax.rem(mine + i, group)
        remote(msgs.at[p], back.at[mine], pb_send, pb_recv,
               {"node": lax.div(p, NY), "local": lax.rem(p, NY)})
        return 0

    for i in range(1, group):
        give(i, 0)
    await_bytes(back.at[pl.ds(0, group - 1)], pb_recv)
    sums = jnp.concatenate(
        [jnp.sum(back[e * NY:(e + 1) * NY], axis=0)[0:1] for e in range(NX)]
        + [jnp.zeros((8 - NX, 128), F32)], axis=0)
    slot_hot = jnp.where(sid == rows_w, 1.0, 0.0)
    got = jnp.dot(sums, slot_hot, preferred_element_type=F32, precision=lax.Precision.HIGHEST)
    total = jnp.sum(jnp.where(eid == lax.broadcasted_iota(jnp.int32, (8, T), 0), got, 0.0),
                    axis=0, keepdims=True)
    dp_ref[...] = total

    await_bytes(wbuf.at[pl.ds(0, ROUNDS + sum(count))], yf_send)
    for r in range(ROUNDS):
        await_bytes(wbuf.at[pl.ds(0, NZ + up[r] + down[r])], ring_send.at[r])
    await_bytes(sendx, xs_sem)
    await_bytes(tok.at[:, pl.ds(CP, CP)], sw_send)
    await_bytes(rets, rt_send)
    await_bytes(outs.at[pl.ds(0, 2 * (NY - 1))], out_send)
    await_bytes(back.at[pl.ds(0, group - 1)], pb_send)


def body(NX, NY, NZ, grad_out, probs, expert_ids, slot_ids, w_down, hidden):
    T, D = grad_out.shape
    ff, BL = w_down.shape[1:]
    cells = hidden.shape[2]
    group = NX * NY
    per = cells // group
    NB, NI = NY // 2, NY // 4
    C0 = NX * per
    CP = -(-(C0 + NX) // 16) * 16
    vm = pl.BlockSpec(memory_space=pltpu.VMEM)
    anym = pl.BlockSpec(memory_space=pl.ANY)
    V, DMA = pltpu.VMEM, pltpu.SemaphoreType.DMA
    dh, dpr = pl.pallas_call(
        functools.partial(kernel, NX, NY, NZ, per, BL),
        out_shape=(jax.ShapeDtypeStruct((cells, ff // NY), BF), jax.ShapeDtypeStruct((1, T), F32)),
        in_specs=[anym, vm, vm, vm, anym, anym],
        out_specs=(vm, vm),
        scratch_shapes=[
            V((T, D), BF), V((ff, BL), BF), V((cells, ff // NY), BF),
            V((NX - 1, NY, 48, BL), BF), V((NY, NX, 48, BL), BF),
            V((NB, CP, BL), BF), V((NB, 2 * CP, BL), BF),
            V((ROUNDS * 2 * NZ, NB - 1, NI * 128 // NZ, BL), BF),
            V((2 * ROUNDS, CP, NI * 128), BF), V((2 * ROUNDS, CP, NI * 128), BF),
            V((2, CP, NI * 128), F32), V((2 * ROUNDS * NI, CP, 128), BF),
            V((2 * NY, CP, 128), BF), V((CP, 128), BF), V((cells, NY * CP), BF),
            V((cells, 128), F32), V((cells, 128), F32),
            V((group, 8, 128), F32), V((group, 8, 128), F32),
            DMA((3,)), DMA, DMA((ROUNDS,)), DMA((ROUNDS * NZ * (NB - 1),)), DMA((ROUNDS,)), DMA, DMA((2,)),
            DMA, DMA, DMA, DMA((2 * ROUNDS,)), DMA, DMA((2,)), DMA, DMA,
        ],
        compiler_params=pltpu.CompilerParams(
            collective_id=0, has_side_effects=True, vmem_limit_bytes=58 * 1024 * 1024),
        cost_estimate=pl.CostEstimate(flops=2 * ff * cells * BL, bytes_accessed=8 << 20,
                                      transcendentals=0),
    )(grad_out, expert_ids.reshape(1, T), slot_ids.reshape(1, T), probs.reshape(1, T),
      w_down[0], hidden[0].T)
    return dh.T[None], dpr[0]


def solution(mesh):
    NX, NY, NZ = mesh.shape["node"], mesh.shape["local"], mesh.shape["dp"] // 2
    return jax.shard_map(
        functools.partial(body, NX, NY, NZ),
        mesh=mesh,
        in_specs=(
            P(("dp", "node", "local"), None),
            P(("dp", "node", "local")),
            P(("dp", "node", "local")),
            P(("dp", "node", "local")),
            P("node", None, "local"),
            P(("dp", "node"), "local", None),
        ),
        out_specs=(P(("dp", "node"), "local", None), P(("dp", "node", "local"))),
        check_vma=False,
    )
```
